32 devices in a mesh: dp: 8 (over z, core), ctx: 4 (over y, x).
Axes of the slice: x: 2, y: 2, z: 4, core: 2. Of those that a mesh axis runs over, the one named last changes fastest.
Arguments:
- q_rows: bfloat16 [16384, 2048], P(('dp', 'ctx')), may hold values from -8 to 8
- kv_rows: bfloat16 [16384, 1024], P(('dp', 'ctx')), may hold values from -8 to 8
- packed_slot: int32 [16384], P(('dp', 'ctx')), may hold values from 0 to 16383, as said below
- doc_ids: int32 [8, 2048], P('dp', 'ctx'), may hold values from 0 to 5, never falling along the last dimension, each value on 1 to 1024 neighbouring positions
Outputs:
- attended: bfloat16 [16384, 2048], P(('dp', 'ctx'))
The draws below stay inside these ranges and needn't reach their ends.
Inputs may be any that keep to these rules, and one draw needn't show every extreme that they name: `packed_slot`: A permutation of the packed positions; the 512 loader rows of every device send exactly 16 rows to the packed positions of each device, position p lying on device p // 512 in the order of dp+ctx. `doc_ids`: document numbers never fall along a sequence; a document has 1 to 1024 positions.
All inputs are finite; a program needn't handle non-finite values.
Results may differ from the reference program's by a relative error of at most 0.0038.
Values may be sent and summed in bfloat16 or wider, within the bound.
No kernel may reach another device: no remote copies, remote signals or barrier semaphores. Data moves between devices by JAX's collectives and lax.ppermute only.
A program may use at most 192 MiB of HBM per device.

```python
import math
import jax
import jax.numpy as jnp
import numpy as np
from jax import lax

HEADS = 16
KV_HEADS = 4
HD = 128
TOK_DEV = 512
DOCS = 6
GROUP = 4
PACK = 2048
ALL = 16384
DOC_MAX = 1024
N_DP = 8
N_CTX = 4


def draw_kv_rows(key, part):
    own_key = jax.random.fold_in(key, 3)
    width = 2 * KV_HEADS * HD
    return jnp.clip(jax.random.normal(own_key, (ALL, width), jnp.float32), -6.0, 6.0).astype(jnp.bfloat16)


def draw_q_rows(key, part):
    own_key = jax.random.fold_in(key, 5)
    width = HEADS * HD
    return jnp.clip(jax.random.normal(own_key, (ALL, width), jnp.float32), -6.0, 6.0).astype(jnp.bfloat16)


def draw_packed_slot(key, part):
    devices = N_DP * N_CTX
    sends = TOK_DEV // devices
    key_local, key_route, key_place = jax.random.split(jax.random.fold_in(key, 29), 3)
    local_order = jax.vmap(lambda sub_key: jax.random.permutation(sub_key, TOK_DEV))(jax.random.split(key_local, devices))
    route = jax.vmap(lambda sub_key: jax.random.permutation(sub_key, devices))(jax.random.split(key_route, devices))
    place = jax.vmap(lambda sub_key: jax.random.permutation(sub_key, TOK_DEV))(jax.random.split(key_place, devices))
    source = jnp.arange(devices, dtype=jnp.int32)[:, None]
    target = jnp.take_along_axis(route, local_order // sends, axis=1)
    inside = place[target, source * sends + local_order % sends]
    return (target * TOK_DEV + inside).reshape(devices * TOK_DEV).astype(jnp.int32)


def length_profile(count, total, most, slope):
    weights = [(1 << 20) // math.isqrt(grade ** slope) + 1 for grade in range(2, count + 1)]
    rest, holding = total - most - (count - 1), [1] * (count - 1)
    while rest > 0:
        candidates = [i for i in range(count - 1) if holding[i] < most]
        mass, budget = sum([weights[i] for i in candidates]), rest
        for i in candidates:
            addition = min(most - holding[i], max(1, budget * weights[i] // mass), rest)
            holding[i] = holding[i] + addition
            rest = rest - addition
    return np.array([most] + holding)


def ragged_sizes(rng, count, total, most, slope):
    if count == 2:
        one = jax.random.randint(rng, (), max(1, total - most), min(most, total - 1) + 1)
        return jnp.stack([one, total - one])
    lengths = jnp.asarray(length_profile(count, total, most, slope), jnp.int32)
    twos = (count - 1) // 2
    donor, taker = lengths[1:1 + 2 * twos:2], lengths[2:2 + 2 * twos:2]
    margin = jnp.minimum(donor - 1, most - taker)
    shifted = jax.random.randint(jax.random.fold_in(rng, 1), (twos,), 0, 1 << 20) % (margin + 1)
    lengths = lengths.at[1:1 + 2 * twos:2].set(donor - shifted).at[2:2 + 2 * twos:2].set(taker + shifted)
    return lengths[jax.random.permutation(jax.random.fold_in(rng, 2), count)]


def setup_inputs(seed: int = 0) -> dict:
    splits = jax.random.split(jax.random.key(seed), 5)
    q_rows = draw_q_rows(jax.random.fold_in(splits[4], 71), 0)
    kv_rows = draw_kv_rows(jax.random.fold_in(splits[4], 71), 0)
    packed_slot = draw_packed_slot(jax.random.fold_in(splits[4], 71), 0)
    doc_ids = jax.vmap(lambda own: jnp.searchsorted(jnp.cumsum(ragged_sizes(own, DOCS, PACK, DOC_MAX, 2)), jnp.arange(PACK), side="right"))(jax.random.split(splits[3], N_DP)).reshape((N_DP, PACK)).astype(jnp.int32)
    return {"q_rows": q_rows, "kv_rows": kv_rows, "packed_slot": packed_slot, "doc_ids": doc_ids}


neg_big = -1e+30

def reference(q_rows, kv_rows, packed_slot, doc_ids):
    q_packed = jnp.zeros_like(q_rows).at[packed_slot].set(q_rows)
    kv_packed = jnp.zeros_like(kv_rows).at[packed_slot].set(kv_rows)
    inv_scale = 1.0 / jnp.sqrt(jnp.float32(HD))
    positions = jnp.arange(PACK, dtype=jnp.int32)
    causal = positions[None, :] <= positions[:, None]

    def one_group(items):
        q_group, kv_group, doc_group = items
        allowed = causal & (doc_group[:, None] == doc_group[None, :])
        queries = q_group.astype(jnp.float32).reshape(PACK, KV_HEADS, GROUP, HD).transpose(1, 2, 0, 3)
        keys = kv_group[:, :KV_HEADS * HD].astype(jnp.float32).reshape(PACK, KV_HEADS, HD).transpose(1, 0, 2)
        values = kv_group[:, KV_HEADS * HD:].astype(jnp.float32).reshape(PACK, KV_HEADS, HD).transpose(1, 0, 2)

        def one_head(parts):
            query_head, key_head, value_head = parts
            scores = jnp.einsum('gtd,pd->gtp', query_head, key_head) * inv_scale
            scores = jnp.where(allowed[None], scores, neg_big)
            largest = lax.optimization_barrier(jnp.max(scores, axis=-1))
            weights = jnp.where(allowed[None], jnp.exp(scores - largest[..., None]), 0.0)
            denominator = lax.optimization_barrier(jnp.sum(weights, axis=-1))
            probs = lax.optimization_barrier(weights.astype(jnp.bfloat16)).astype(jnp.float32)
            summed = jnp.einsum('gtp,pd->gtd', probs, value_head)
            return summed / denominator[..., None]
        heads_out = lax.map(one_head, (queries, keys, values))
        return heads_out.transpose(2, 0, 1, 3).reshape(PACK, HEADS * HD).astype(jnp.bfloat16)
    grouped = lax.map(one_group, (q_packed.reshape(N_DP, PACK, HEADS * HD), kv_packed.reshape(N_DP, PACK, 2 * KV_HEADS * HD), doc_ids))
    return grouped.reshape(ALL, HEADS * HD)
```

```python
import functools
import math

import jax
import jax.numpy as jnp
from jax import lax
from jax.experimental import pallas as pl
from jax.experimental.pallas import tpu as pltpu
from jax.sharding import PartitionSpec as P

HEADS = 16
KV_HEADS = 4
HD = 128
GROUP = 4
KV_COLS = 2 * KV_HEADS * HD
GROUP_COLS = GROUP * HD
META = 128
Q_TILE = 128
K_STEP = 256
NEG = -1e30
MIB = 1 << 20

F32 = jnp.float32
BF16 = jnp.bfloat16


def dot(a, b):
    return jnp.dot(a, b, preferred_element_type=F32)


def dot_nt(a, b):
    return lax.dot_general(a, b, (((1,), (1,)), ((), ())), preferred_element_type=F32)


def iota(shape, dim):
    return lax.broadcasted_iota(jnp.int32, shape, dim)


def send_matrix(slot, devices):
    rows = slot.shape[1]
    target = slot // rows
    one_hot = (iota((devices, rows), 0) == target).astype(F32)
    before = (iota((rows, rows), 0) < iota((rows, rows), 1)).astype(BF16)
    rank = jnp.sum(dot(one_hot.astype(BF16), before) * one_hot, axis=0, keepdims=True)
    where_to = target * (rows // devices) + rank.astype(jnp.int32)
    return (iota((rows, rows), 0) == where_to).astype(BF16)


def pack_kv_kernel(devices, slot_ref, kv_ref, out_ref):
    slot = slot_ref[...]
    rows = slot.shape[1]
    matrix = send_matrix(slot, devices)
    local = slot % rows
    which = iota((META, rows), 0)
    digits = jnp.where(which == 0, local // 16, jnp.where(which == 1, local % 16, 0))
    out_ref[:, :KV_COLS] = dot(matrix, kv_ref[...]).astype(BF16)
    out_ref[:, KV_COLS:] = dot_nt(matrix, digits.astype(BF16)).astype(BF16)


def pack_q_kernel(devices, slot_ref, q_ref, out_ref, matrix_ref):
    @pl.when(pl.program_id(0) == 0)
    def _():
        matrix_ref[...] = send_matrix(slot_ref[...], devices)

    out_ref[...] = dot(matrix_ref[...], q_ref[...]).astype(BF16)


def sort_kv_kernel(got_ref, out_ref, place_ref):
    rows = got_ref.shape[0]
    pick = (iota((8, META), 0) == iota((8, META), 1)).astype(BF16)
    digits = dot_nt(pick, got_ref[:, KV_COLS:])
    place = (digits[0:1] * 16 + digits[1:2]).astype(jnp.int32)
    place_ref[...] = place
    matrix = (iota((rows, rows), 0) == place).astype(BF16)
    out_ref[...] = dot(matrix, got_ref[:, :KV_COLS]).astype(BF16)


def attend_kernel(blocks, steps_ref, place_ref, start_ref, q_ref, *refs):
    key_refs, value_refs = refs[:blocks], refs[blocks : 2 * blocks]
    out_ref, matrix_ref, bias_ref, q_buf, key_buf, value_buf = refs[2 * blocks :]
    rows = q_ref.shape[0]
    width = key_buf.shape[0]
    pad = width - blocks * rows
    scale = math.log2(math.e) / math.sqrt(HD)

    @pl.when(pl.program_id(0) == 0)
    def _():
        matrix_ref[...] = (iota((rows, rows), 0) == place_ref[...]).astype(BF16)
        column = iota((rows, width), 1)
        last = iota((rows, 1), 0) + (width - rows)
        allowed = (column >= start_ref[...] + pad) & (column <= last)
        bias_ref[...] = jnp.where(allowed, 0.0, NEG)
        key_buf[:pad, :] = jnp.zeros((pad, HD), BF16)
        value_buf[:pad, :HD] = jnp.zeros((pad, HD), BF16)
        value_buf[:, HD:] = jnp.ones((width, HD), BF16)

    q_buf[...] = dot(matrix_ref[...], q_ref[...]).astype(BF16)
    for b in range(blocks):
        key_buf[pl.ds(pad + b * rows, rows), :] = key_refs[b][...]
        value_buf[pl.ds(pad + b * rows, rows), :HD] = value_refs[b][...]

    @pl.loop(0, rows // Q_TILE)
    def _(tile):
        here = pl.ds(pl.multiple_of(tile * Q_TILE, Q_TILE), Q_TILE)
        end = (width - rows) + (tile + 1) * Q_TILE

        def run(steps):
            span = steps * K_STEP
            keys = pl.ds(pl.multiple_of(end - span, Q_TILE), span)
            bias = bias_ref[here, keys]
            queries = jnp.concatenate(
                [q_buf[here, h * HD : (h + 1) * HD] for h in range(GROUP)], axis=0
            )
            scores = dot_nt(queries, key_buf[keys, :])
            scores = scores.reshape(GROUP, Q_TILE, span) + bias[None]
            largest = jnp.max(scores, axis=-1, keepdims=True)
            probs = jnp.exp2((scores - largest) * scale).astype(BF16)
            summed = dot(probs.reshape(GROUP * Q_TILE, span), value_buf[keys, :])
            result = (summed[:, :HD] / summed[:, HD:]).astype(BF16)
            for h in range(GROUP):
                out_ref[here, h * HD : (h + 1) * HD] = result[h * Q_TILE : (h + 1) * Q_TILE]

        for steps in range(1, -(-(width - pad) // K_STEP) + 1):
            pl.when(steps_ref[tile] == steps)(functools.partial(run, steps))


def all_to_all(x):
    return lax.all_to_all(x, ("dp", "ctx"), split_axis=0, concat_axis=0, tiled=True)


def per_device(q_rows, kv_rows, packed_slot, doc_ids):
    rows = q_rows.shape[0]
    ctx_size = lax.axis_size("ctx")
    devices = lax.axis_size("dp") * ctx_size
    pack = rows * ctx_size
    doc_max = pack // 2
    before = min(ctx_size - 1, -(-(doc_max - 1) // rows))
    blocks = before + 1
    slot = packed_slot.reshape(1, rows)
    params = pltpu.CompilerParams(vmem_limit_bytes=48 * MIB)

    kv_out = pl.pallas_call(
        functools.partial(pack_kv_kernel, devices),
        out_shape=jax.ShapeDtypeStruct((rows, KV_COLS + META), BF16),
        compiler_params=params,
        name="pack_kv",
    )(slot, kv_rows)
    kv_got = all_to_all(kv_out)

    q_out = pl.pallas_call(
        functools.partial(pack_q_kernel, devices),
        out_shape=jax.ShapeDtypeStruct(q_rows.shape, BF16),
        grid=(KV_HEADS,),
        in_specs=[
            pl.BlockSpec((1, rows), lambda g: (0, 0)),
            pl.BlockSpec((rows, GROUP_COLS), lambda g: (0, g)),
        ],
        out_specs=pl.BlockSpec((rows, GROUP_COLS), lambda g: (0, g)),
        scratch_shapes=[pltpu.VMEM((rows, rows), BF16)],
        compiler_params=params,
        name="pack_q",
    )(slot, q_rows)
    q_got = all_to_all(q_out)

    kv_here, place = pl.pallas_call(
        sort_kv_kernel,
        out_shape=(
            jax.ShapeDtypeStruct((rows, KV_COLS), BF16),
            jax.ShapeDtypeStruct((1, rows), jnp.int32),
        ),
        compiler_params=params,
        name="sort_kv",
    )(kv_got)

    def from_before(x, distance):
        return lax.ppermute(x, "ctx", [(i, i + distance) for i in range(ctx_size - distance)])

    docs = doc_ids.reshape(rows) + 1
    doc_line = jnp.concatenate([from_before(docs, d) for d in range(before, 0, -1)] + [docs])
    start = jnp.sum((doc_line[None, :] < docs[:, None]).astype(jnp.int32), axis=1)
    ends = before * rows + jnp.arange(Q_TILE, rows + 1, Q_TILE, dtype=jnp.int32)
    steps = (ends - start[::Q_TILE] + K_STEP - 1) // K_STEP

    kv_blocks = [from_before(kv_here, d) for d in range(before, 0, -1)] + [kv_here]

    width = Q_TILE + blocks * rows
    whole = lambda shape: pl.BlockSpec(shape, lambda g, s: (0, 0))
    return pl.pallas_call(
        functools.partial(attend_kernel, blocks),
        out_shape=jax.ShapeDtypeStruct(q_rows.shape, BF16),
        grid_spec=pltpu.PrefetchScalarGridSpec(
            num_scalar_prefetch=1,
            grid=(KV_HEADS,),
            in_specs=[whole((1, rows)), whole((rows, 1))]
            + [pl.BlockSpec((rows, GROUP_COLS), lambda g, s: (0, g))]
            + [pl.BlockSpec((rows, HD), lambda g, s: (0, g))] * blocks
            + [pl.BlockSpec((rows, HD), lambda g, s: (0, KV_HEADS + g))] * blocks,
            out_specs=pl.BlockSpec((rows, GROUP_COLS), lambda g, s: (0, g)),
            scratch_shapes=[
                pltpu.VMEM((rows, rows), BF16),
                pltpu.VMEM((rows, width), F32),
                pltpu.VMEM((rows, GROUP_COLS), BF16),
                pltpu.VMEM((width, HD), BF16),
                pltpu.VMEM((width, 2 * HD), BF16),
            ],
        ),
        compiler_params=params,
        name="attend",
    )(steps, place, start.reshape(rows, 1), q_got, *kv_blocks, *kv_blocks)


def solution(mesh):
    return jax.shard_map(
        per_device,
        mesh=mesh,
        in_specs=(P(("dp", "ctx"), None), P(("dp", "ctx"), None), P(("dp", "ctx")), P("dp", "ctx")),
        out_specs=P(("dp", "ctx"), None),
        check_vma=False,
    )
```

```python
import functools
import math

import jax
import jax.numpy as jnp
from jax import lax
from jax.experimental import pallas as pl
from jax.experimental.pallas import tpu as pltpu
from jax.sharding import PartitionSpec as P

HEADS = 16
KV_HEADS = 4
HD = 128
GROUP = 4
KV_COLS = 2 * KV_HEADS * HD
GROUP_COLS = GROUP * HD
META = 128
STEP = 256
NEG = -1e30
MIB = 1 << 20

F32 = jnp.float32
BF16 = jnp.bfloat16


def dot(a, b):
    return jnp.dot(a, b, preferred_element_type=F32)


def dot_nt(a, b):
    return lax.dot_general(a, b, (((1,), (1,)), ((), ())), preferred_element_type=F32)


def iota(shape, dim):
    return lax.broadcasted_iota(jnp.int32, shape, dim)


def send_matrix(slot, devices):
    rows = slot.shape[1]
    target = slot // rows
    one_hot = (iota((devices, rows), 0) == target).astype(F32)
    before = (iota((rows, rows), 0) < iota((rows, rows), 1)).astype(BF16)
    rank = jnp.sum(dot(one_hot.astype(BF16), before) * one_hot, axis=0, keepdims=True)
    where_to = target * (rows // devices) + rank.astype(jnp.int32)
    return (iota((rows, rows), 0) == where_to).astype(BF16)


def pack_kv_kernel(devices, slot_ref, kv_ref, out_ref):
    slot = slot_ref[...]
    rows = slot.shape[1]
    matrix = send_matrix(slot, devices)
    local = slot % rows
    which = iota((META, rows), 0)
    digits = jnp.where(which == 0, local // 16, jnp.where(which == 1, local % 16, 0))
    out_ref[:, :KV_COLS] = dot(matrix, kv_ref[...]).astype(BF16)
    out_ref[:, KV_COLS:] = dot_nt(matrix, digits.astype(BF16)).astype(BF16)


def pack_q_kernel(devices, slot_ref, q_ref, out_ref, matrix_ref):
    @pl.when(pl.program_id(0) == 0)
    def _():
        matrix_ref[...] = send_matrix(slot_ref[...], devices)

    out_ref[...] = dot(matrix_ref[...], q_ref[...]).astype(BF16)


def sort_kv_kernel(got_ref, key_ref, value_ref, place_ref):
    rows = got_ref.shape[0]
    half = KV_HEADS * HD
    pick = (iota((8, META), 0) == iota((8, META), 1)).astype(BF16)
    digits = dot_nt(pick, got_ref[:, KV_COLS:])
    place = (digits[0:1] * 16 + digits[1:2]).astype(jnp.int32)
    place_ref[...] = place
    matrix = (iota((rows, rows), 0) == place).astype(BF16)
    key_ref[...] = dot(matrix, got_ref[:, :half]).astype(BF16)
    value_ref[...] = dot(matrix, got_ref[:, half:KV_COLS]).astype(BF16).T


def attend_kernel(parts, early_ref, place_ref, start_ref, q_ref, *refs):
    count = sum(parts)
    key_refs, value_refs = refs[:count], refs[count : 2 * count]
    out_ref, matrix_ref, bias_ref, q_buf, key_buf, value_buf, score_buf = refs[2 * count :]
    rows = q_ref.shape[0]
    width = key_buf.shape[0]
    begin = width - rows
    scale = math.log2(math.e) / math.sqrt(HD)
    first, early_steps, all_early = early_ref[0], early_ref[1], early_ref[2]

    @pl.when(pl.program_id(0) == 0)
    def _():
        matrix_ref[...] = (iota((rows, rows), 0) == place_ref[...]).astype(BF16)
        key, query = iota((rows, rows), 0), iota((rows, rows), 1)
        allowed = (key + begin >= start_ref[...]) & (key <= query)
        bias_ref[...] = jnp.where(allowed, 0.0, NEG)
        value_buf[HD:, :] = jnp.ones((value_buf.shape[0] - HD, width), BF16)

    q_buf[...] = dot(matrix_ref[...], q_ref[...]).astype(BF16)
    for b, n in enumerate(parts):
        at, here = sum(parts[:b]), slice(b * rows, (b + 1) * rows)
        key_buf[here, :] = sum([ref[...] for ref in key_refs[at + 1 : at + n]], key_refs[at][...])
        value_buf[:HD, here] = sum([ref[...] for ref in value_refs[at + 1 : at + n]], value_refs[at][...])

    def run(counts):
        def steps_of(tile):
            return list(range(begin - counts[tile] * STEP, begin + (tile + 1) * STEP, STEP))

        def queries_of(tile):
            return slice(tile * STEP, (tile + 1) * STEP)

        def score(slot, tile, h, i, at, tops):
            part = dot_nt(
                key_buf[at : at + STEP, :], q_buf[queries_of(tile), h * HD : (h + 1) * HD]
            )
            own = at >= begin
            if own:
                part = part + bias_ref[at - begin : at - begin + STEP, queries_of(tile)]
            elif i == 0:
                part = jnp.where(iota((STEP, 1), 0) + at >= first, part, NEG)
            score_buf[slot, i * STEP : (i + 1) * STEP, :] = part
            peak = jnp.max(part.reshape(STEP // 8, 8, STEP), axis=0)
            tops[own] = jnp.maximum(tops[own], peak) if own in tops else peak

        def largest_of(tile, tops):
            own = jnp.max(tops[True], axis=0, keepdims=True)
            if False not in tops:
                return {True: own}
            shared = jnp.where(start_ref[:, queries_of(tile)] == first, 0.0, -NEG)
            early = jnp.max(tops[False], axis=0, keepdims=True)
            both = jnp.maximum(own, early - shared)
            return {True: both, False: both + shared}

        def weigh(slot, i, at, largest, summed):
            part = score_buf[slot, i * STEP : (i + 1) * STEP, :]
            probs = jnp.exp2((part - largest[at >= begin]) * scale).astype(BF16)
            added = dot(value_buf[:, at : at + STEP], probs)
            return added if summed is None else summed + added

        def finish(tile, h, summed):
            result = (summed[:HD] * (1.0 / summed[HD : HD + 1])).astype(BF16)
            out_ref[queries_of(tile), h * HD : (h + 1) * HD] = result.T

        chains = [(tile, h) for tile in range(rows // STEP) for h in range(GROUP)]
        largest = {}
        for c in range(len(chains) + 1):
            tops, summed = {}, None
            now = steps_of(chains[c][0]) if c < len(chains) else []
            past = steps_of(chains[c - 1][0]) if c else []
            for i in range(max(len(now), len(past))):
                if i < len(now):
                    score(c % 2, *chains[c], i, now[i], tops)
                if i < len(past):
                    summed = weigh((c - 1) % 2, i, past[i], largest[c - 1], summed)
            if now:
                largest[c] = largest_of(chains[c][0], tops)
            if past:
                finish(*chains[c - 1], summed)

    tiles = rows // STEP
    for early in range(begin // STEP + 1):
        for whole in (False, True) if early else (True,):
            counts = [early if whole or t == 0 else 0 for t in range(tiles)]
            pl.when((early_steps == early) & (all_early == int(whole)))(functools.partial(run, counts))


def all_to_all(x):
    return lax.all_to_all(x, ("dp", "ctx"), split_axis=0, concat_axis=0, tiled=True)


def attend(early, place, start, q_got, keys, values):
    rows = q_got.shape[0]
    parts = [len(block) for block in keys]
    blocks = len(parts)
    keys, values = sum(keys, []), sum(values, [])
    width = blocks * rows
    whole = lambda shape: pl.BlockSpec(shape, lambda g, *_: (0, 0))
    return pl.pallas_call(
        functools.partial(attend_kernel, parts),
        out_shape=jax.ShapeDtypeStruct(q_got.shape, BF16),
        grid_spec=pltpu.PrefetchScalarGridSpec(
            num_scalar_prefetch=1,
            grid=(KV_HEADS,),
            in_specs=[whole((1, rows)), whole((1, rows))]
            + [pl.BlockSpec((rows, GROUP_COLS), lambda g, *_: (0, g))]
            + [pl.BlockSpec((rows, HD), lambda g, *_: (0, g))] * len(keys)
            + [pl.BlockSpec((HD, rows), lambda g, *_: (g, 0))] * len(keys),
            out_specs=pl.BlockSpec((rows, GROUP_COLS), lambda g, *_: (0, g)),
            scratch_shapes=[
                pltpu.VMEM((rows, rows), BF16),
                pltpu.VMEM((rows, rows), F32),
                pltpu.VMEM((rows, GROUP_COLS), BF16),
                pltpu.VMEM((width, HD), BF16),
                pltpu.VMEM((HD + 16, width), BF16),
                pltpu.VMEM((2, width, STEP), F32),
            ],
        ),
        compiler_params=pltpu.CompilerParams(vmem_limit_bytes=48 * MIB),
        name="attend",
    )(early, place, start.reshape(1, rows), q_got, *keys, *values)


def per_device(q_rows, kv_rows, packed_slot, doc_ids):
    rows = q_rows.shape[0]
    ctx_size = lax.axis_size("ctx")
    devices = lax.axis_size("dp") * ctx_size
    pack = rows * ctx_size
    doc_max = pack // 2
    before = min(ctx_size - 1, -(-(doc_max - 1) // rows))
    blocks = before + 1
    slot = packed_slot.reshape(1, rows)
    params = pltpu.CompilerParams(vmem_limit_bytes=48 * MIB)

    kv_out = pl.pallas_call(
        functools.partial(pack_kv_kernel, devices),
        out_shape=jax.ShapeDtypeStruct((rows, KV_COLS + META), BF16),
        compiler_params=params,
        name="pack_kv",
    )(slot, kv_rows)
    kv_got = all_to_all(kv_out)

    q_out = pl.pallas_call(
        functools.partial(pack_q_kernel, devices),
        out_shape=jax.ShapeDtypeStruct(q_rows.shape, BF16),
        grid=(KV_HEADS,),
        in_specs=[
            pl.BlockSpec((1, rows), lambda g: (0, 0)),
            pl.BlockSpec((rows, GROUP_COLS), lambda g: (0, g)),
        ],
        out_specs=pl.BlockSpec((rows, GROUP_COLS), lambda g: (0, g)),
        scratch_shapes=[pltpu.VMEM((rows, rows), BF16)],
        compiler_params=params,
        name="pack_q",
    )(slot, q_rows)
    q_got = all_to_all(q_out)

    keys, values, place = pl.pallas_call(
        sort_kv_kernel,
        out_shape=(
            jax.ShapeDtypeStruct((rows, KV_HEADS * HD), BF16),
            jax.ShapeDtypeStruct((KV_HEADS * HD, rows), BF16),
            jax.ShapeDtypeStruct((1, rows), jnp.int32),
        ),
        compiler_params=params,
        name="sort_kv",
    )(kv_got)

    def from_before(x, distance):
        return lax.ppermute(x, "ctx", [(i, i + distance) for i in range(ctx_size - distance)])

    docs = doc_ids.reshape(rows) + 1
    doc_line = jnp.concatenate([from_before(docs, d) for d in range(before, 0, -1)] + [docs])
    start = jnp.sum((doc_line[None, :] < docs[:, None]).astype(jnp.int32), axis=1)
    begin = before * rows
    first = start[0]
    early_steps = jnp.maximum(begin - first + STEP - 1, 0) // STEP
    all_early = (start[rows - STEP] == first) | (early_steps == 0)
    early = jnp.stack([first, early_steps, all_early.astype(jnp.int32)])

    def spread(x):
        if ctx_size == 4 and before == 2:
            near = lax.ppermute(x, "ctx", [(0, 1), (2, 3)])
            far = lax.ppermute(x, "ctx", [(0, 2), (1, 3)])
            return [[far], [near, lax.ppermute(far, "ctx", [(3, 2)])], [x]]
        return [[from_before(x, d)] for d in range(before, 0, -1)] + [[x]]

    keys, values = spread(keys), spread(values)
    return attend(early, place, start, q_got, keys, values)


def solution(mesh):
    return jax.shard_map(
        per_device,
        mesh=mesh,
        in_specs=(P(("dp", "ctx"), None), P(("dp", "ctx"), None), P(("dp", "ctx")), P("dp", "ctx")),
        out_specs=P(("dp", "ctx"), None),
        check_vma=False,
    )
```

```python
import functools
import math

import jax
import jax.numpy as jnp
from jax import lax
from jax.experimental import pallas as pl
from jax.experimental.pallas import tpu as pltpu
from jax.sharding import PartitionSpec as P

HEADS = 16
KV_HEADS = 4
HD = 128
GROUP = 4
KV_COLS = 2 * KV_HEADS * HD
GROUP_COLS = GROUP * HD
META = 128
STEP = 256
NEG = -1e30
MIB = 1 << 20

F32 = jnp.float32
BF16 = jnp.bfloat16


def dot(a, b):
    return jnp.dot(a, b, preferred_element_type=F32)


def dot_nt(a, b):
    return lax.dot_general(a, b, (((1,), (1,)), ((), ())), preferred_element_type=F32)


def iota(shape, dim):
    return lax.broadcasted_iota(jnp.int32, shape, dim)


def send_matrix(slot, devices):
    rows = slot.shape[1]
    target = slot // rows
    one_hot = (iota((devices, rows), 0) == target).astype(F32)
    before = (iota((rows, rows), 0) < iota((rows, rows), 1)).astype(BF16)
    rank = jnp.sum(dot(one_hot.astype(BF16), before) * one_hot, axis=0, keepdims=True)
    where_to = target * (rows // devices) + rank.astype(jnp.int32)
    return (iota((rows, rows), 0) == where_to).astype(BF16)


def pack_kv_kernel(devices, slot_ref, kv_hbm, out_ref, kv_ref, sem):
    copy = pltpu.make_async_copy(kv_hbm, kv_ref, sem)
    copy.start()
    slot = slot_ref[...]
    rows = slot.shape[1]
    matrix = send_matrix(slot, devices)
    local = slot % rows
    which = iota((META, rows), 0)
    digits = jnp.where(which == 0, local // 16, jnp.where(which == 1, local % 16, 0))
    out_ref[:, KV_COLS:] = dot_nt(matrix, digits.astype(BF16)).astype(BF16)
    copy.wait()
    out_ref[:, :KV_COLS] = dot(matrix, kv_ref[...]).astype(BF16)


def pack_q_kernel(devices, slot_ref, q_ref, out_ref, matrix_ref):
    @pl.when(pl.program_id(0) == 0)
    def _():
        matrix_ref[...] = send_matrix(slot_ref[...], devices)

    out_ref[...] = dot(matrix_ref[...], q_ref[...]).astype(BF16)


def sort_kv_kernel(got_ref, place_ref, kv_ref, *piece_refs):
    rows = got_ref.shape[0]
    half = KV_HEADS * HD
    pick = (iota((8, META), 0) == iota((8, META), 1)).astype(BF16)
    digits = dot_nt(pick, got_ref[:, KV_COLS:])
    place = (digits[0:1] * 16 + digits[1:2]).astype(jnp.int32)
    place_ref[...] = place
    matrix = (iota((rows, rows), 0) == place).astype(BF16)
    kv_ref[:rows, :] = dot(matrix, got_ref[:, :half]).astype(BF16)
    kv_ref[rows:, :] = dot(matrix, got_ref[:, half:KV_COLS]).astype(BF16).T
    at = 0
    for piece_ref in piece_refs:
        piece_ref[...] = kv_ref[at : at + piece_ref.shape[0], :]
        at += piece_ref.shape[0]


def attend_kernel(sources, early_ref, place_ref, start_ref, q_ref, *refs):
    kv_refs = refs[:-7]
    out_ref, matrix_ref, bias_ref, q_buf, key_buf, value_buf, score_buf = refs[-7:]
    rows = q_ref.shape[0]
    width = key_buf.shape[0]
    begin = width - rows
    scale = math.log2(math.e) / math.sqrt(HD)
    first, early_steps, all_early = early_ref[0], early_ref[1], early_ref[2]

    @pl.when(pl.program_id(0) == 0)
    def _():
        matrix_ref[...] = (iota((rows, rows), 0) == place_ref[...]).astype(BF16)
        key, query = iota((rows, rows), 0), iota((rows, rows), 1)
        allowed = (key + begin >= start_ref[...]) & (key <= query)
        bias_ref[...] = jnp.where(allowed, 0.0, NEG)
        value_buf[HD:, :] = jnp.ones((value_buf.shape[0] - HD, width), BF16)

    q_buf[...] = dot(matrix_ref[...], q_ref[...]).astype(BF16)
    group, at = pl.program_id(0), 0
    for b, block in enumerate(sources):
        keys, values = [], []
        for count in block:
            refs_here = kv_refs[at : at + count]
            at += count
            if count == 2:
                key, value = (ref[...] for ref in refs_here)
            else:
                key = jnp.concatenate([ref[...] for ref in refs_here[:2]], axis=0)
                value = jnp.where(group < KV_HEADS // 2, refs_here[2][...], refs_here[3][...])
            keys.append(key)
            values.append(value)
        here = slice(b * rows, (b + 1) * rows)
        key_buf[here, :] = sum(keys[1:], keys[0])
        value_buf[:HD, here] = sum(values[1:], values[0])

    def run(counts):
        def steps_of(tile):
            return list(range(begin - counts[tile] * STEP, begin + (tile + 1) * STEP, STEP))

        def queries_of(tile):
            return slice(tile * STEP, (tile + 1) * STEP)

        def score(slot, tile, h, i, at, tops):
            part = dot_nt(
                key_buf[at : at + STEP, :], q_buf[queries_of(tile), h * HD : (h + 1) * HD]
            )
            own = at >= begin
            if own:
                part = part + bias_ref[at - begin : at - begin + STEP, queries_of(tile)]
            elif i == 0:
                part = jnp.where(iota((STEP, 1), 0) + at >= first, part, NEG)
            score_buf[slot, i * STEP : (i + 1) * STEP, :] = part
            peak = jnp.max(part.reshape(STEP // 8, 8, STEP), axis=0)
            tops[own] = jnp.maximum(tops[own], peak) if own in tops else peak

        def largest_of(tile, tops):
            own = jnp.max(tops[True], axis=0, keepdims=True)
            if False not in tops:
                return {True: own}
            shared = jnp.where(start_ref[:, queries_of(tile)] == first, 0.0, -NEG)
            early = jnp.max(tops[False], axis=0, keepdims=True)
            both = jnp.maximum(own, early - shared)
            return {True: both, False: both + shared}

        def weigh(slot, i, at, largest, summed):
            part = score_buf[slot, i * STEP : (i + 1) * STEP, :]
            probs = jnp.exp2((part - largest[at >= begin]) * scale).astype(BF16)
            added = dot(value_buf[:, at : at + STEP], probs)
            return added if summed is None else summed + added

        def finish(tile, h, summed):
            result = (summed[:HD] * (1.0 / summed[HD : HD + 1])).astype(BF16)
            out_ref[queries_of(tile), h * HD : (h + 1) * HD] = result.T

        chains = [(tile, h) for tile in range(rows // STEP) for h in range(GROUP)]
        largest = {}
        for c in range(len(chains) + 1):
            tops, summed = {}, None
            now = steps_of(chains[c][0]) if c < len(chains) else []
            past = steps_of(chains[c - 1][0]) if c else []
            for i in range(max(len(now), len(past))):
                if i < len(now):
                    score(c % 2, *chains[c], i, now[i], tops)
                if i < len(past):
                    summed = weigh((c - 1) % 2, i, past[i], largest[c - 1], summed)
            if now:
                largest[c] = largest_of(chains[c][0], tops)
            if past:
                finish(*chains[c - 1], summed)

    tiles = rows // STEP
    for early in range(begin // STEP + 1):
        for whole in (False, True) if early else (True,):
            counts = [early if whole or t == 0 else 0 for t in range(tiles)]
            pl.when((early_steps == early) & (all_early == int(whole)))(functools.partial(run, counts))


def all_to_all(x):
    return lax.all_to_all(x, ("dp", "ctx"), split_axis=0, concat_axis=0, tiled=True)


def attend(early, place, start, q_got, kv):
    rows = q_got.shape[0]
    blocks = len(kv)
    width = blocks * rows
    keys_of = pl.BlockSpec((rows, HD), lambda g, *_: (0, g))
    values_of = pl.BlockSpec((HD, rows), lambda g, *_: (rows // HD + g, 0))
    keys_of_half = pl.BlockSpec((rows // 2, HD), lambda g, *_: (0, g))
    values_of_half = pl.BlockSpec((HD, rows), lambda g, *_: (g % (KV_HEADS // 2), 0))
    arrays, specs = [], []
    for block in kv:
        for source in block:
            one = len(source) == 1
            arrays += list(source) * 2 if one else list(source)
            specs += [keys_of, values_of] if one else [keys_of_half] * 2 + [values_of_half] * 2
    sources = [[2 if len(source) == 1 else 4 for source in block] for block in kv]
    whole = lambda shape: pl.BlockSpec(shape, lambda g, *_: (0, 0))
    return pl.pallas_call(
        functools.partial(attend_kernel, sources),
        out_shape=jax.ShapeDtypeStruct(q_got.shape, BF16),
        grid_spec=pltpu.PrefetchScalarGridSpec(
            num_scalar_prefetch=1,
            grid=(KV_HEADS,),
            in_specs=[whole((1, rows)), whole((1, rows))]
            + [pl.BlockSpec((rows, GROUP_COLS), lambda g, *_: (0, g))]
            + specs,
            out_specs=pl.BlockSpec((rows, GROUP_COLS), lambda g, *_: (0, g)),
            scratch_shapes=[
                pltpu.VMEM((rows, rows), BF16),
                pltpu.VMEM((rows, rows), F32),
                pltpu.VMEM((rows, GROUP_COLS), BF16),
                pltpu.VMEM((width, HD), BF16),
                pltpu.VMEM((HD + 16, width), BF16),
                pltpu.VMEM((2, width, STEP), F32),
            ],
        ),
        compiler_params=pltpu.CompilerParams(vmem_limit_bytes=62 * MIB),
        name="attend",
    )(early, place, start, q_got, *arrays)


def per_device(q_rows, kv_rows, packed_slot, doc_ids):
    rows = q_rows.shape[0]
    ctx_size = lax.axis_size("ctx")
    devices = lax.axis_size("dp") * ctx_size
    pack = rows * ctx_size
    doc_max = pack // 2
    before = min(ctx_size - 1, -(-(doc_max - 1) // rows))
    blocks = before + 1
    slot = packed_slot.reshape(1, rows)
    params = pltpu.CompilerParams(vmem_limit_bytes=48 * MIB)

    kv_out = pl.pallas_call(
        functools.partial(pack_kv_kernel, devices),
        out_shape=jax.ShapeDtypeStruct((rows, KV_COLS + META), BF16),
        in_specs=[pl.BlockSpec(memory_space=pltpu.VMEM), pl.BlockSpec(memory_space=pl.ANY)],
        scratch_shapes=[pltpu.VMEM(kv_rows.shape, BF16), pltpu.SemaphoreType.DMA],
        compiler_params=pltpu.CompilerParams(vmem_limit_bytes=60 * MIB),
        name="pack_kv",
    )(slot, kv_rows)

    def from_before(x, distance):
        return lax.ppermute(x, "ctx", [(i, i + distance) for i in range(ctx_size - distance)])

    kv_out, docs = lax.optimization_barrier((kv_out, doc_ids.reshape(rows) + 1))
    kv_got = all_to_all(kv_out)

    doc_line = jnp.concatenate([from_before(docs, d) for d in range(before, 0, -1)] + [docs])
    start = jnp.sum((doc_line[None, :] < docs[:, None]).astype(jnp.int32), axis=1)
    begin = before * rows
    first = start[0]
    early_steps = jnp.maximum(begin - first + STEP - 1, 0) // STEP
    all_early = (start[rows - STEP] == first) | (early_steps == 0)
    early = jnp.stack([first, early_steps, all_early.astype(jnp.int32)])
    q_rows, early, start = lax.optimization_barrier((q_rows, early, start.reshape(1, rows)))

    q_out = pl.pallas_call(
        functools.partial(pack_q_kernel, devices),
        out_shape=jax.ShapeDtypeStruct(q_rows.shape, BF16),
        grid=(KV_HEADS,),
        in_specs=[
            pl.BlockSpec((1, rows), lambda g: (0, 0)),
            pl.BlockSpec((rows, GROUP_COLS), lambda g: (0, g)),
        ],
        out_specs=pl.BlockSpec((rows, GROUP_COLS), lambda g: (0, g)),
        scratch_shapes=[pltpu.VMEM((rows, rows), BF16)],
        compiler_params=params,
        name="pack_q",
    )(slot, q_rows)
    q_got = all_to_all(q_out)

    relay = ctx_size == 4 and before == 2
    pieces = (rows // 2, rows // 2, KV_HEADS // 2 * HD, KV_HEADS // 2 * HD) if relay else ()
    place, kv_here, *pieces = pl.pallas_call(
        sort_kv_kernel,
        out_shape=[jax.ShapeDtypeStruct((1, rows), jnp.int32)]
        + [jax.ShapeDtypeStruct((n, rows), BF16) for n in (rows + KV_HEADS * HD, *pieces)],
        compiler_params=params,
        name="sort_kv",
    )(kv_got)

    if relay:
        far = [lax.ppermute(x, "ctx", [(0, 2), (1, 3)]) for x in pieces]
        near = lax.ppermute(kv_here, "ctx", [(0, 1), (2, 3)])
        hop = [lax.ppermute(x, "ctx", [(3, 2)]) for x in far]
        kv = [[far], [[near], hop], [[kv_here]]]
    else:
        kv = [[[from_before(kv_here, d)]] for d in range(before, 0, -1)] + [[[kv_here]]]
    return attend(early, place, start, q_got, kv)


def solution(mesh):
    return jax.shard_map(
        per_device,
        mesh=mesh,
        in_specs=(P(("dp", "ctx"), None), P(("dp", "ctx"), None), P(("dp", "ctx")), P("dp", "ctx")),
        out_specs=P(("dp", "ctx"), None),
        check_vma=False,
    )
```

```python
import functools
import math

import jax
import jax.numpy as jnp
from jax import lax
from jax.experimental import pallas as pl
from jax.experimental.pallas import tpu as pltpu
from jax.sharding import PartitionSpec as P

HEADS = 16
KV_HEADS = 4
HD = 128
GROUP = 4
KV_COLS = 2 * KV_HEADS * HD
GROUP_COLS = GROUP * HD
META = 128
STEP = 256
VMEM_ATTEND = 62
NEG = -1e30
MIB = 1 << 20

F32 = jnp.float32
BF16 = jnp.bfloat16


def dot(a, b):
    return jnp.dot(a, b, preferred_element_type=F32)


def dot_nt(a, b):
    return lax.dot_general(a, b, (((1,), (1,)), ((), ())), preferred_element_type=F32)


def iota(shape, dim):
    return lax.broadcasted_iota(jnp.int32, shape, dim)


def send_matrix(slot, devices):
    rows = slot.shape[1]
    target = slot // rows
    one_hot = (iota((devices, rows), 0) == target).astype(F32)
    before = (iota((rows, rows), 0) < iota((rows, rows), 1)).astype(BF16)
    rank = jnp.sum(dot(one_hot.astype(BF16), before) * one_hot, axis=0, keepdims=True)
    where_to = target * (rows // devices) + rank.astype(jnp.int32)
    return (iota((rows, rows), 0) == where_to).astype(BF16)


def pack_kv_kernel(devices, slot_ref, kv_hbm, out_ref, kv_ref, sem):
    copy = pltpu.make_async_copy(kv_hbm, kv_ref, sem)
    copy.start()
    slot = slot_ref[...]
    rows = slot.shape[1]
    matrix = send_matrix(slot, devices)
    local = slot % rows
    which = iota((META, rows), 0)
    digits = jnp.where(which == 0, local // 16, jnp.where(which == 1, local % 16, 0))
    out_ref[:, KV_COLS:] = dot_nt(matrix, digits.astype(BF16)).astype(BF16)
    copy.wait()
    out_ref[:, :KV_COLS] = dot(matrix, kv_ref[...]).astype(BF16)


def pack_q_kernel(devices, slot_ref, q_ref, out_ref, matrix_ref):
    @pl.when(pl.program_id(0) == 0)
    def _():
        matrix_ref[...] = send_matrix(slot_ref[...], devices)

    out_ref[...] = dot(matrix_ref[...], q_ref[...]).astype(BF16)


def sort_kv_kernel(got_ref, place_ref, kv_ref, *piece_refs):
    rows = got_ref.shape[0]
    half = KV_HEADS * HD
    pick = (iota((8, META), 0) == iota((8, META), 1)).astype(BF16)
    digits = dot_nt(pick, got_ref[:, KV_COLS:])
    place = (digits[0:1] * 16 + digits[1:2]).astype(jnp.int32)
    place_ref[...] = place
    matrix = (iota((rows, rows), 0) == place).astype(BF16)
    kv_ref[:rows, :] = dot(matrix, got_ref[:, :half]).astype(BF16)
    kv_ref[rows:, :] = dot(matrix, got_ref[:, half:KV_COLS]).astype(BF16).T
    at = 0
    for piece_ref in piece_refs:
        piece_ref[...] = kv_ref[at : at + piece_ref.shape[0], :]
        at += piece_ref.shape[0]


def attend_kernel(sources, early_ref, place_ref, start_ref, q_ref, *refs):
    kv_refs = refs[:-7]
    out_ref, bias_ref, q_buf, key_buf, value_buf, even_buf, odd_buf = refs[-7:]
    rows = q_ref.shape[0]
    width = key_buf.shape[0]
    tiles = rows // STEP
    begin = width - rows
    scale = math.log2(math.e) / math.sqrt(HD)
    first, early_steps, all_early = early_ref[0], early_ref[1], early_ref[2]

    matrix = (iota((rows, rows), 0) == place_ref[...]).astype(BF16)
    for g in range(KV_HEADS):
        columns = slice(g * GROUP_COLS, (g + 1) * GROUP_COLS)
        q_buf[:, columns] = dot(matrix, q_ref[:, columns]).astype(BF16)
    key, query = iota((rows, rows), 0), iota((rows, rows), 1)
    allowed = (key + begin >= start_ref[...]) & (key <= query)
    bias_ref[...] = jnp.where(allowed, 0.0, NEG)

    at = 0
    for b, block in enumerate(sources):
        here = slice(b * rows, (b + 1) * rows)
        parts = []
        for count in block:
            parts.append([ref[...] for ref in kv_refs[at : at + count]])
            parts[-1] = jnp.concatenate(parts[-1], axis=0) if count > 1 else parts[-1][0]
            at += count
        kv = sum(parts[1:], parts[0])
        key_buf[here, :] = kv[:rows]
        for g in range(KV_HEADS):
            value_buf[g, :HD, here] = kv[rows + g * HD : rows + (g + 1) * HD]
    for g in range(KV_HEADS):
        value_buf[g, HD:, :] = jnp.ones((value_buf.shape[1] - HD, width), BF16)

    def run(counts):
        def steps_of(tile):
            return list(range(begin - counts[tile] * STEP, begin + (tile + 1) * STEP, STEP))

        def queries_of(tile):
            return slice(tile * STEP, (tile + 1) * STEP)

        def columns(index):
            return pl.ds(pl.multiple_of(index * HD, HD), HD)

        def score(buf, head, tile, i, at, tops):
            part = dot_nt(
                key_buf[at : at + STEP, columns(head // GROUP)],
                q_buf[queries_of(tile), columns(head)],
            )
            own = at >= begin
            if own:
                part = part + bias_ref[at - begin : at - begin + STEP, queries_of(tile)]
            elif i == 0:
                part = jnp.where(iota((STEP, 1), 0) + at >= first, part, NEG)
            buf[tile, i * STEP : (i + 1) * STEP, :] = part
            peak = jnp.max(part.reshape(STEP // 8, 8, STEP), axis=0)
            tops[own] = jnp.maximum(tops[own], peak) if own in tops else peak

        def largest_of(tile, tops):
            own = jnp.max(tops[True], axis=0, keepdims=True)
            if False not in tops:
                return own, own
            shared = jnp.where(start_ref[:, queries_of(tile)] == first, 0.0, -NEG)
            early = jnp.max(tops[False], axis=0, keepdims=True)
            both = jnp.maximum(own, early - shared)
            return both, both + shared

        def weigh(buf, head, tile, i, at, largest, summed):
            part = buf[tile, i * STEP : (i + 1) * STEP, :]
            probs = jnp.exp2((part - largest[int(at < begin)]) * scale).astype(BF16)
            added = dot(value_buf[head // GROUP, :, at : at + STEP], probs)
            return added if summed is None else summed + added

        def finish(head, tile, summed):
            result = (summed[:HD] * (1.0 / summed[HD : HD + 1])).astype(BF16)
            out_ref[queries_of(tile), columns(head)] = result.T

        def both(next_buf, next_head, buf, head, largest):
            coming = []
            for tile in range(tiles):
                tops, summed = {}, None
                for i, at in enumerate(steps_of(tile)):
                    if head is not None:
                        summed = weigh(buf, head, tile, i, at, largest[tile], summed)
                    score(next_buf, next_head, tile, i, at, tops)
                if head is not None:
                    finish(head, tile, summed)
                coming.append(largest_of(tile, tops))
            return tuple(coming)

        def two_heads(pair, largest):
            head = 2 * pair
            largest = both(odd_buf, head + 1, even_buf, head, largest)
            return both(even_buf, jnp.minimum(head + 2, HEADS - 1), odd_buf, head + 1, largest)

        lax.fori_loop(0, HEADS // 2, two_heads, both(even_buf, 0, None, None, None))

    for early in range(begin // STEP + 1):
        for whole in (False, True) if early else (True,):
            counts = [early if whole or t == 0 else 0 for t in range(tiles)]
            pl.when((early_steps == early) & (all_early == int(whole)))(functools.partial(run, counts))


def all_to_all(x):
    return lax.all_to_all(x, ("dp", "ctx"), split_axis=0, concat_axis=0, tiled=True)


def attend(early, place, start, q_got, kv):
    rows = q_got.shape[0]
    width = len(kv) * rows
    arrays = [x for block in kv for source in block for x in source]
    return pl.pallas_call(
        functools.partial(attend_kernel, [[len(source) for source in block] for block in kv]),
        out_shape=jax.ShapeDtypeStruct(q_got.shape, BF16),
        in_specs=[pl.BlockSpec(memory_space=pltpu.SMEM)]
        + [pl.BlockSpec(memory_space=pltpu.VMEM)] * (3 + len(arrays)),
        scratch_shapes=[
            pltpu.VMEM((rows, rows), F32),
            pltpu.VMEM(q_got.shape, BF16),
            pltpu.VMEM((width, KV_HEADS * HD), BF16),
            pltpu.VMEM((KV_HEADS, HD + 16, width), BF16),
            pltpu.VMEM((rows // STEP, width, STEP), F32),
            pltpu.VMEM((rows // STEP, width, STEP), F32),
        ],
        compiler_params=pltpu.CompilerParams(vmem_limit_bytes=VMEM_ATTEND * MIB),
        name="attend",
    )(early, place, start, q_got, *arrays)


def per_device(q_rows, kv_rows, packed_slot, doc_ids):
    rows = q_rows.shape[0]
    ctx_size = lax.axis_size("ctx")
    devices = lax.axis_size("dp") * ctx_size
    pack = rows * ctx_size
    doc_max = pack // 2
    before = min(ctx_size - 1, -(-(doc_max - 1) // rows))
    blocks = before + 1
    slot = packed_slot.reshape(1, rows)
    params = pltpu.CompilerParams(vmem_limit_bytes=48 * MIB)

    kv_out = pl.pallas_call(
        functools.partial(pack_kv_kernel, devices),
        out_shape=jax.ShapeDtypeStruct((rows, KV_COLS + META), BF16),
        in_specs=[pl.BlockSpec(memory_space=pltpu.VMEM), pl.BlockSpec(memory_space=pl.ANY)],
        scratch_shapes=[pltpu.VMEM(kv_rows.shape, BF16), pltpu.SemaphoreType.DMA],
        compiler_params=pltpu.CompilerParams(vmem_limit_bytes=60 * MIB),
        name="pack_kv",
    )(slot, kv_rows)

    def from_before(x, distance):
        return lax.ppermute(x, "ctx", [(i, i + distance) for i in range(ctx_size - distance)])

    kv_out, docs = lax.optimization_barrier((kv_out, doc_ids))
    kv_got = all_to_all(kv_out)
    docs = docs.reshape(rows) + 1

    doc_line = jnp.concatenate([from_before(docs, d) for d in range(before, 0, -1)] + [docs])
    start = jnp.sum((doc_line[None, :] < docs[:, None]).astype(jnp.int32), axis=1)
    begin = before * rows
    first = start[0]
    early_steps = jnp.maximum(begin - first + STEP - 1, 0) // STEP
    all_early = (start[rows - STEP] == first) | (early_steps == 0)
    early = jnp.stack([first, early_steps, all_early.astype(jnp.int32)])
    q_rows, early, start = lax.optimization_barrier((q_rows, early, start.reshape(1, rows)))

    q_out = pl.pallas_call(
        functools.partial(pack_q_kernel, devices),
        out_shape=jax.ShapeDtypeStruct(q_rows.shape, BF16),
        grid=(KV_HEADS,),
        in_specs=[
            pl.BlockSpec((1, rows), lambda g: (0, 0)),
            pl.BlockSpec((rows, GROUP_COLS), lambda g: (0, g)),
        ],
        out_specs=pl.BlockSpec((rows, GROUP_COLS), lambda g: (0, g)),
        scratch_shapes=[pltpu.VMEM((rows, rows), BF16)],
        compiler_params=params,
        name="pack_q",
    )(slot, q_rows)
    q_got = all_to_all(q_out)

    relay = ctx_size == 4 and before == 2
    pieces = (rows // 2, rows // 2, KV_HEADS // 2 * HD, KV_HEADS // 2 * HD) if relay else ()
    place, kv_here, *pieces = pl.pallas_call(
        sort_kv_kernel,
        out_shape=[jax.ShapeDtypeStruct((1, rows), jnp.int32)]
        + [jax.ShapeDtypeStruct((n, rows), BF16) for n in (rows + KV_HEADS * HD, *pieces)],
        compiler_params=params,
        name="sort_kv",
    )(kv_got)

    if relay:
        far = [lax.ppermute(x, "ctx", [(0, 2), (1, 3)]) for x in pieces]
        near = lax.ppermute(kv_here, "ctx", [(0, 1), (2, 3)])
        hop = [lax.ppermute(x, "ctx", [(3, 2)]) for x in far]
        kv = [[far], [[near], hop], [[kv_here]]]
    else:
        kv = [[[from_before(kv_here, d)]] for d in range(before, 0, -1)] + [[[kv_here]]]
    return attend(early, place, start, q_got, kv)


def solution(mesh):
    return jax.shard_map(
        per_device,
        mesh=mesh,
        in_specs=(P(("dp", "ctx"), None), P(("dp", "ctx"), None), P(("dp", "ctx")), P("dp", "ctx")),
        out_specs=P(("dp", "ctx"), None),
        check_vma=False,
    )
```

```python
import functools
import math

import jax
import jax.numpy as jnp
from jax import lax
from jax.experimental import pallas as pl
from jax.experimental.pallas import tpu as pltpu
from jax.sharding import PartitionSpec as P

HEADS = 16
KV_HEADS = 4
HD = 128
GROUP = 4
KV_COLS = 2 * KV_HEADS * HD
GROUP_COLS = GROUP * HD
META = 128
STEP = 256
VMEM_ATTEND = 62
NEG = -1e30
MIB = 1 << 20

F32 = jnp.float32
BF16 = jnp.bfloat16


def dot(a, b):
    return jnp.dot(a, b, preferred_element_type=F32)


def dot_nt(a, b):
    return lax.dot_general(a, b, (((1,), (1,)), ((), ())), preferred_element_type=F32)


def iota(shape, dim):
    return lax.broadcasted_iota(jnp.int32, shape, dim)


def send_matrix(slot, devices):
    rows = slot.shape[1]
    target = slot // rows
    one_hot = (iota((devices, rows), 0) == target).astype(F32)
    before = (iota((rows, rows), 0) < iota((rows, rows), 1)).astype(BF16)
    rank = jnp.sum(dot(one_hot.astype(BF16), before) * one_hot, axis=0, keepdims=True)
    where_to = target * (rows // devices) + rank.astype(jnp.int32)
    return (iota((rows, rows), 0) == where_to).astype(BF16)


def pack_kv_kernel(devices, slot_ref, kv_hbm, out_ref, kv_ref, sem):
    copy = pltpu.make_async_copy(kv_hbm, kv_ref, sem)
    copy.start()
    slot = slot_ref[...]
    rows = slot.shape[1]
    matrix = send_matrix(slot, devices)
    local = slot % rows
    which = iota((META, rows), 0)
    digits = jnp.where(which == 0, local // 16, jnp.where(which == 1, local % 16, 0))
    out_ref[:, KV_COLS:] = dot_nt(matrix, digits.astype(BF16)).astype(BF16)
    copy.wait()
    out_ref[:, :KV_COLS] = dot(matrix, kv_ref[...]).astype(BF16)


def pack_q_kernel(devices, slot_ref, q_ref, out_ref, matrix_ref):
    @pl.when(pl.program_id(0) == 0)
    def _():
        matrix_ref[...] = send_matrix(slot_ref[...], devices)

    out_ref[...] = dot(matrix_ref[...], q_ref[...]).astype(BF16)


def sort_kv_kernel(got_ref, place_ref, kv_ref, *piece_refs):
    rows = got_ref.shape[0]
    half = KV_HEADS * HD
    pick = (iota((8, META), 0) == iota((8, META), 1)).astype(BF16)
    digits = dot_nt(pick, got_ref[:, KV_COLS:])
    place = (digits[0:1] * 16 + digits[1:2]).astype(jnp.int32)
    place_ref[...] = place
    matrix = (iota((rows, rows), 0) == place).astype(BF16)
    kv_ref[:rows, :] = dot(matrix, got_ref[:, :half]).astype(BF16)
    kv_ref[rows:, :] = dot(matrix, got_ref[:, half:KV_COLS]).astype(BF16).T
    at = 0
    for piece_ref in piece_refs:
        piece_ref[...] = kv_ref[at : at + piece_ref.shape[0], :]
        at += piece_ref.shape[0]


def attend_kernel(sources, early_ref, place_ref, start_ref, q_ref, *refs):
    kv_refs = refs[:-7]
    out_ref, bias_ref, q_buf, key_buf, value_buf, even_buf, odd_buf = refs[-7:]
    rows = q_ref.shape[0]
    width = key_buf.shape[0]
    tiles = rows // STEP
    begin = width - rows
    scale = math.log2(math.e) / math.sqrt(HD)
    first, early_steps, all_early = early_ref[0], early_ref[1], early_ref[2]

    matrix = (iota((rows, rows), 0) == place_ref[...]).astype(BF16)
    for g in range(KV_HEADS):
        columns = slice(g * GROUP_COLS, (g + 1) * GROUP_COLS)
        q_buf[:, columns] = dot(matrix, q_ref[:, columns]).astype(BF16)
    key, query = iota((rows, rows), 0), iota((rows, rows), 1)
    allowed = (key + begin >= start_ref[...]) & (key <= query)
    bias_ref[...] = jnp.where(allowed, 0.0, NEG)

    at = 0
    for b, block in enumerate(sources):
        here = slice(b * rows, (b + 1) * rows)
        parts = []
        for count in block:
            parts.append([ref[...] for ref in kv_refs[at : at + count]])
            parts[-1] = jnp.concatenate(parts[-1], axis=0) if count > 1 else parts[-1][0]
            at += count
        kv = sum(parts[1:], parts[0])
        key_buf[here, :] = kv[:rows]
        for g in range(KV_HEADS):
            value_buf[g, :HD, here] = kv[rows + g * HD : rows + (g + 1) * HD]
    for g in range(KV_HEADS):
        value_buf[g, HD:, :] = jnp.ones((value_buf.shape[1] - HD, width), BF16)

    def run(counts):
        def steps_of(tile):
            return list(range(begin - counts[tile] * STEP, begin + (tile + 1) * STEP, STEP))

        def queries_of(tile):
            return slice(tile * STEP, (tile + 1) * STEP)

        def columns(index):
            return pl.ds(pl.multiple_of(index * HD, HD), HD)

        def score(buf, head, tile, i, at, tops):
            part = dot_nt(
                key_buf[at : at + STEP, columns(head // GROUP)],
                q_buf[queries_of(tile), columns(head)],
            )
            own = at >= begin
            if own:
                part = part + bias_ref[at - begin : at - begin + STEP, queries_of(tile)]
            elif i == 0:
                part = jnp.where(iota((STEP, 1), 0) + at >= first, part, NEG)
            buf[tile, i * STEP : (i + 1) * STEP, :] = part
            peak = jnp.max(part.reshape(STEP // 8, 8, STEP), axis=0)
            tops[own] = jnp.maximum(tops[own], peak) if own in tops else peak

        def largest_of(tile, tops):
            own = jnp.max(tops[True], axis=0, keepdims=True)
            if False not in tops:
                return own, own
            shared = jnp.where(start_ref[:, queries_of(tile)] == first, 0.0, -NEG)
            early = jnp.max(tops[False], axis=0, keepdims=True)
            both = jnp.maximum(own, early - shared)
            return both, both + shared

        def weigh(buf, head, tile, i, at, largest, summed):
            part = buf[tile, i * STEP : (i + 1) * STEP, :]
            probs = jnp.exp2((part - largest[int(at < begin)]) * scale).astype(BF16)
            added = dot(value_buf[head // GROUP, :, at : at + STEP], probs)
            return added if summed is None else summed + added

        def finish(head, tile, summed):
            result = (summed[:HD] * (1.0 / summed[HD : HD + 1])).astype(BF16)
            out_ref[queries_of(tile), columns(head)] = result.T

        def both(next_buf, next_head, buf, head, largest):
            coming = []
            for tile in range(tiles):
                tops, summed = {}, None
                for i, at in enumerate(steps_of(tile)):
                    if head is not None:
                        summed = weigh(buf, head, tile, i, at, largest[tile], summed)
                    score(next_buf, next_head, tile, i, at, tops)
                if head is not None:
                    finish(head, tile, summed)
                coming.append(largest_of(tile, tops))
            return tuple(coming)

        def two_heads(pair, largest):
            head = 2 * pair
            largest = both(odd_buf, head + 1, even_buf, head, largest)
            return both(even_buf, jnp.minimum(head + 2, HEADS - 1), odd_buf, head + 1, largest)

        lax.fori_loop(
            0, HEADS // 2, two_heads, both(even_buf, 0, None, None, None), unroll=2
        )

    for early in range(begin // STEP + 1):
        for whole in (False, True) if early else (True,):
            counts = [early if whole or t == 0 else 0 for t in range(tiles)]
            pl.when((early_steps == early) & (all_early == int(whole)))(functools.partial(run, counts))


def all_to_all(x):
    return lax.all_to_all(x, ("dp", "ctx"), split_axis=0, concat_axis=0, tiled=True)


def attend(early, place, start, q_got, kv):
    rows = q_got.shape[0]
    width = len(kv) * rows
    arrays = [x for block in kv for source in block for x in source]
    return pl.pallas_call(
        functools.partial(attend_kernel, [[len(source) for source in block] for block in kv]),
        out_shape=jax.ShapeDtypeStruct(q_got.shape, BF16),
        in_specs=[pl.BlockSpec(memory_space=pltpu.SMEM)]
        + [pl.BlockSpec(memory_space=pltpu.VMEM)] * (3 + len(arrays)),
        scratch_shapes=[
            pltpu.VMEM((rows, rows), F32),
            pltpu.VMEM(q_got.shape, BF16),
            pltpu.VMEM((width, KV_HEADS * HD), BF16),
            pltpu.VMEM((KV_HEADS, HD + 16, width), BF16),
            pltpu.VMEM((rows // STEP, width, STEP), F32),
            pltpu.VMEM((rows // STEP, width, STEP), F32),
        ],
        compiler_params=pltpu.CompilerParams(vmem_limit_bytes=VMEM_ATTEND * MIB),
        name="attend",
    )(early, place, start, q_got, *arrays)


def per_device(q_rows, kv_rows, packed_slot, doc_ids):
    rows = q_rows.shape[0]
    ctx_size = lax.axis_size("ctx")
    devices = lax.axis_size("dp") * ctx_size
    pack = rows * ctx_size
    doc_max = pack // 2
    before = min(ctx_size - 1, -(-(doc_max - 1) // rows))
    blocks = before + 1
    slot = packed_slot.reshape(1, rows)
    params = pltpu.CompilerParams(vmem_limit_bytes=48 * MIB)

    kv_out = pl.pallas_call(
        functools.partial(pack_kv_kernel, devices),
        out_shape=jax.ShapeDtypeStruct((rows, KV_COLS + META), BF16),
        in_specs=[pl.BlockSpec(memory_space=pltpu.VMEM), pl.BlockSpec(memory_space=pl.ANY)],
        scratch_shapes=[pltpu.VMEM(kv_rows.shape, BF16), pltpu.SemaphoreType.DMA],
        compiler_params=pltpu.CompilerParams(vmem_limit_bytes=60 * MIB),
        name="pack_kv",
    )(slot, kv_rows)

    def from_before(x, distance):
        return lax.ppermute(x, "ctx", [(i, i + distance) for i in range(ctx_size - distance)])

    kv_out, docs = lax.optimization_barrier((kv_out, doc_ids))
    kv_got = all_to_all(kv_out)
    docs = docs.reshape(rows) + 1

    doc_line = jnp.concatenate([from_before(docs, d) for d in range(before, 0, -1)] + [docs])
    start = jnp.sum((doc_line[None, :] < docs[:, None]).astype(jnp.int32), axis=1)
    begin = before * rows
    first = start[0]
    early_steps = jnp.maximum(begin - first + STEP - 1, 0) // STEP
    all_early = (start[rows - STEP] == first) | (early_steps == 0)
    early = jnp.stack([first, early_steps, all_early.astype(jnp.int32)])
    q_rows, early, start = lax.optimization_barrier((q_rows, early, start.reshape(1, rows)))

    q_out = pl.pallas_call(
        functools.partial(pack_q_kernel, devices),
        out_shape=jax.ShapeDtypeStruct(q_rows.shape, BF16),
        grid=(KV_HEADS,),
        in_specs=[
            pl.BlockSpec((1, rows), lambda g: (0, 0)),
            pl.BlockSpec((rows, GROUP_COLS), lambda g: (0, g)),
        ],
        out_specs=pl.BlockSpec((rows, GROUP_COLS), lambda g: (0, g)),
        scratch_shapes=[pltpu.VMEM((rows, rows), BF16)],
        compiler_params=params,
        name="pack_q",
    )(slot, q_rows)
    q_got = all_to_all(q_out)

    relay = ctx_size == 4 and before == 2
    pieces = (rows // 2, rows // 2, KV_HEADS // 2 * HD, KV_HEADS // 2 * HD) if relay else ()
    place, kv_here, *pieces = pl.pallas_call(
        sort_kv_kernel,
        out_shape=[jax.ShapeDtypeStruct((1, rows), jnp.int32)]
        + [jax.ShapeDtypeStruct((n, rows), BF16) for n in (rows + KV_HEADS * HD, *pieces)],
        compiler_params=params,
        name="sort_kv",
    )(kv_got)

    if relay:
        far = [lax.ppermute(x, "ctx", [(0, 2), (1, 3)]) for x in pieces]
        near = lax.ppermute(kv_here, "ctx", [(0, 1), (2, 3)])
        hop = [lax.ppermute(x, "ctx", [(3, 2)]) for x in far]
        kv = [[far], [[near], hop], [[kv_here]]]
    else:
        kv = [[[from_before(kv_here, d)]] for d in range(before, 0, -1)] + [[[kv_here]]]
    return attend(early, place, start, q_got, kv)


def solution(mesh):
    return jax.shard_map(
        per_device,
        mesh=mesh,
        in_specs=(P(("dp", "ctx"), None), P(("dp", "ctx"), None), P(("dp", "ctx")), P("dp", "ctx")),
        out_specs=P(("dp", "ctx"), None),
        check_vma=False,
    )
```

```python
import functools
import math

import jax
import jax.numpy as jnp
from jax import lax
from jax.experimental import pallas as pl
from jax.experimental.pallas import tpu as pltpu
from jax.sharding import PartitionSpec as P

HEADS = 16
KV_HEADS = 4
HD = 128
GROUP = 4
KV_COLS = 2 * KV_HEADS * HD
GROUP_COLS = GROUP * HD
META = 128
STEP = 256
VMEM_ATTEND = 63
NEG = -1e30
MIB = 1 << 20

F32 = jnp.float32
BF16 = jnp.bfloat16


def dot(a, b):
    return jnp.dot(a, b, preferred_element_type=F32)


def dot_nt(a, b):
    return lax.dot_general(a, b, (((1,), (1,)), ((), ())), preferred_element_type=F32)


def iota(shape, dim):
    return lax.broadcasted_iota(jnp.int32, shape, dim)


def send_matrix(slot, devices):
    rows = slot.shape[1]
    target = slot // rows
    one_hot = (iota((devices, rows), 0) == target).astype(F32)
    before = (iota((rows, rows), 0) < iota((rows, rows), 1)).astype(BF16)
    rank = jnp.sum(dot(one_hot.astype(BF16), before) * one_hot, axis=0, keepdims=True)
    where_to = target * (rows // devices) + rank.astype(jnp.int32)
    return (iota((rows, rows), 0) == where_to).astype(BF16)


def pack_kv_kernel(devices, slot_ref, kv_hbm, out_ref, kv_ref, sem):
    copy = pltpu.make_async_copy(kv_hbm, kv_ref, sem)
    copy.start()
    slot = slot_ref[...]
    rows = slot.shape[1]
    matrix = send_matrix(slot, devices)
    local = slot % rows
    which = iota((META, rows), 0)
    digits = jnp.where(which == 0, local // 16, jnp.where(which == 1, local % 16, 0))
    out_ref[:, KV_COLS:] = dot_nt(matrix, digits.astype(BF16)).astype(BF16)
    copy.wait()
    out_ref[:, :KV_COLS] = dot(matrix, kv_ref[...]).astype(BF16)


def pack_q_kernel(devices, slot_ref, q_ref, out_ref, matrix_ref):
    @pl.when(pl.program_id(0) == 0)
    def _():
        matrix_ref[...] = send_matrix(slot_ref[...], devices)

    out_ref[...] = dot(matrix_ref[...], q_ref[...]).astype(BF16)


def sort_kv_kernel(got_ref, place_ref, kv_ref, *piece_refs):
    rows = got_ref.shape[0]
    half = KV_HEADS * HD
    pick = (iota((8, META), 0) == iota((8, META), 1)).astype(BF16)
    digits = dot_nt(pick, got_ref[:, KV_COLS:])
    place = (digits[0:1] * 16 + digits[1:2]).astype(jnp.int32)
    place_ref[...] = place
    matrix = (iota((rows, rows), 0) == place).astype(BF16)
    kv_ref[:rows, :] = dot(matrix, got_ref[:, :half]).astype(BF16)
    kv_ref[rows:, :] = dot(matrix, got_ref[:, half:KV_COLS]).astype(BF16).T
    at = 0
    for piece_ref in piece_refs:
        piece_ref[...] = kv_ref[at : at + piece_ref.shape[0], :]
        at += piece_ref.shape[0]


def attend_kernel(sources, early_ref, place_ref, start_ref, q_ref, *refs):
    kv_refs = refs[:-7]
    out_ref, bias_ref, q_buf, key_buf, value_buf, even_buf, odd_buf = refs[-7:]
    rows = q_ref.shape[0]
    width = key_buf.shape[0]
    tiles = rows // STEP
    begin = width - rows
    scale = math.log2(math.e) / math.sqrt(HD)
    first, early_steps, all_early = early_ref[0], early_ref[1], early_ref[2]

    matrix = (iota((rows, rows), 0) == place_ref[...]).astype(BF16)
    for g in range(KV_HEADS):
        columns = slice(g * GROUP_COLS, (g + 1) * GROUP_COLS)
        q_buf[:, columns] = dot(matrix, q_ref[:, columns]).astype(BF16)
    key, query = iota((rows, rows), 0), iota((rows, rows), 1)
    allowed = (key + begin >= start_ref[...]) & (key <= query)
    bias_ref[...] = jnp.where(allowed, 0.0, NEG)

    at = 0
    for b, block in enumerate(sources):
        here = slice(b * rows, (b + 1) * rows)
        parts = []
        for count in block:
            parts.append([ref[...] for ref in kv_refs[at : at + count]])
            parts[-1] = jnp.concatenate(parts[-1], axis=0) if count > 1 else parts[-1][0]
            at += count
        kv = sum(parts[1:], parts[0])
        key_buf[here, :] = kv[:rows]
        for g in range(KV_HEADS):
            value_buf[g, :HD, here] = kv[rows + g * HD : rows + (g + 1) * HD]
    for g in range(KV_HEADS):
        value_buf[g, HD:, :] = jnp.ones((value_buf.shape[1] - HD, width), BF16)

    def run(counts):
        def steps_of(tile):
            return list(range(begin - counts[tile] * STEP, begin + (tile + 1) * STEP, STEP))

        def queries_of(tile):
            return slice(tile * STEP, (tile + 1) * STEP)

        def columns(index):
            return pl.ds(pl.multiple_of(index * HD, HD), HD)

        def score(buf, head, tile, i, at, tops):
            part = dot_nt(
                key_buf[at : at + STEP, columns(head // GROUP)],
                q_buf[queries_of(tile), columns(head)],
            )
            own = at >= begin
            if own:
                part = part + bias_ref[at - begin : at - begin + STEP, queries_of(tile)]
            elif i == 0:
                part = jnp.where(iota((STEP, 1), 0) + at >= first, part, NEG)
            buf[tile, i * STEP : (i + 1) * STEP, :] = part
            peak = jnp.max(part.reshape(STEP // 8, 8, STEP), axis=0)
            tops[own] = jnp.maximum(tops[own], peak) if own in tops else peak

        def largest_of(tile, tops):
            own = jnp.max(tops[True], axis=0, keepdims=True)
            if False not in tops:
                return own, own
            shared = jnp.where(start_ref[:, queries_of(tile)] == first, 0.0, -NEG)
            early = jnp.max(tops[False], axis=0, keepdims=True)
            both = jnp.maximum(own, early - shared)
            return both, both + shared

        def weigh(buf, head, tile, i, at, largest, summed):
            part = buf[tile, i * STEP : (i + 1) * STEP, :]
            probs = jnp.exp2((part - largest[int(at < begin)]) * scale).astype(BF16)
            added = dot(value_buf[head // GROUP, :, at : at + STEP], probs)
            return added if summed is None else summed + added

        def finish(head, tile, summed):
            result = (summed[:HD] * (1.0 / summed[HD : HD + 1])).astype(BF16)
            out_ref[queries_of(tile), columns(head)] = result.T

        def both(next_buf, next_head, buf, head, largest):
            coming = []
            for tile in range(tiles):
                tops, summed = {}, None
                for i, at in enumerate(steps_of(tile)):
                    if head is not None:
                        summed = weigh(buf, head, tile, i, at, largest[tile], summed)
                    score(next_buf, next_head, tile, i, at, tops)
                if head is not None:
                    finish(head, tile, summed)
                coming.append(largest_of(tile, tops))
            return tuple(coming)

        def two_heads(pair, largest):
            head = 2 * pair
            largest = both(odd_buf, head + 1, even_buf, head, largest)
            return both(even_buf, jnp.minimum(head + 2, HEADS - 1), odd_buf, head + 1, largest)

        lax.fori_loop(
            0, HEADS // 2, two_heads, both(even_buf, 0, None, None, None), unroll=2
        )

    for early in range(begin // STEP + 1):
        for whole in (False, True) if early else (True,):
            counts = [early if whole or t == 0 else 0 for t in range(tiles)]
            pl.when((early_steps == early) & (all_early == int(whole)))(functools.partial(run, counts))


def all_to_all(x):
    return lax.all_to_all(x, ("dp", "ctx"), split_axis=0, concat_axis=0, tiled=True)


def attend(early, place, start, q_got, kv):
    rows = q_got.shape[0]
    width = len(kv) * rows
    arrays = [x for block in kv for source in block for x in source]
    return pl.pallas_call(
        functools.partial(attend_kernel, [[len(source) for source in block] for block in kv]),
        out_shape=jax.ShapeDtypeStruct(q_got.shape, BF16),
        in_specs=[pl.BlockSpec(memory_space=pltpu.SMEM)]
        + [pl.BlockSpec(memory_space=pltpu.VMEM)] * (3 + len(arrays)),
        scratch_shapes=[
            pltpu.VMEM((rows, rows), F32),
            pltpu.VMEM(q_got.shape, BF16),
            pltpu.VMEM((width, KV_HEADS * HD), BF16),
            pltpu.VMEM((KV_HEADS, HD + 16, width), BF16),
            pltpu.VMEM((rows // STEP, width, STEP), F32),
            pltpu.VMEM((rows // STEP, width, STEP), F32),
        ],
        compiler_params=pltpu.CompilerParams(vmem_limit_bytes=VMEM_ATTEND * MIB),
        name="attend",
    )(early, place, start, q_got, *arrays)


def per_device(q_rows, kv_rows, packed_slot, doc_ids):
    rows = q_rows.shape[0]
    ctx_size = lax.axis_size("ctx")
    devices = lax.axis_size("dp") * ctx_size
    pack = rows * ctx_size
    doc_max = pack // 2
    before = min(ctx_size - 1, -(-(doc_max - 1) // rows))
    blocks = before + 1
    slot = packed_slot.reshape(1, rows)
    params = pltpu.CompilerParams(vmem_limit_bytes=48 * MIB)

    kv_out = pl.pallas_call(
        functools.partial(pack_kv_kernel, devices),
        out_shape=jax.ShapeDtypeStruct((rows, KV_COLS + META), BF16),
        in_specs=[pl.BlockSpec(memory_space=pltpu.VMEM), pl.BlockSpec(memory_space=pl.ANY)],
        scratch_shapes=[pltpu.VMEM(kv_rows.shape, BF16), pltpu.SemaphoreType.DMA],
        compiler_params=pltpu.CompilerParams(vmem_limit_bytes=60 * MIB),
        name="pack_kv",
    )(slot, kv_rows)

    def from_before(x, distance):
        return lax.ppermute(x, "ctx", [(i, i + distance) for i in range(ctx_size - distance)])

    kv_out, docs = lax.optimization_barrier((kv_out, doc_ids))
    kv_got = all_to_all(kv_out)
    docs = docs.reshape(rows) + 1

    doc_line = jnp.concatenate([from_before(docs, d) for d in range(before, 0, -1)] + [docs])
    start = jnp.sum((doc_line[None, :] < docs[:, None]).astype(jnp.int32), axis=1)
    begin = before * rows
    first = start[0]
    early_steps = jnp.maximum(begin - first + STEP - 1, 0) // STEP
    all_early = (start[rows - STEP] == first) | (early_steps == 0)
    early = jnp.stack([first, early_steps, all_early.astype(jnp.int32)])
    q_rows, early, start = lax.optimization_barrier((q_rows, early, start.reshape(1, rows)))

    q_out = pl.pallas_call(
        functools.partial(pack_q_kernel, devices),
        out_shape=jax.ShapeDtypeStruct(q_rows.shape, BF16),
        grid=(KV_HEADS,),
        in_specs=[
            pl.BlockSpec((1, rows), lambda g: (0, 0)),
            pl.BlockSpec((rows, GROUP_COLS), lambda g: (0, g)),
        ],
        out_specs=pl.BlockSpec((rows, GROUP_COLS), lambda g: (0, g)),
        scratch_shapes=[pltpu.VMEM((rows, rows), BF16)],
        compiler_params=params,
        name="pack_q",
    )(slot, q_rows)
    q_got = all_to_all(q_out)

    relay = ctx_size == 4 and before == 2
    pieces = (rows // 2, rows // 2, KV_HEADS // 2 * HD, KV_HEADS // 2 * HD) if relay else ()
    place, kv_here, *pieces = pl.pallas_call(
        sort_kv_kernel,
        out_shape=[jax.ShapeDtypeStruct((1, rows), jnp.int32)]
        + [jax.ShapeDtypeStruct((n, rows), BF16) for n in (rows + KV_HEADS * HD, *pieces)],
        compiler_params=params,
        name="sort_kv",
    )(kv_got)

    if relay:
        far = [lax.ppermute(x, "ctx", [(0, 2), (1, 3)]) for x in pieces]
        near = lax.ppermute(kv_here, "ctx", [(0, 1), (2, 3)])
        hop = [lax.ppermute(x, "ctx", [(3, 2)]) for x in far]
        kv = [[far], [[near], hop], [[kv_here]]]
    else:
        kv = [[[from_before(kv_here, d)]] for d in range(before, 0, -1)] + [[[kv_here]]]
    return attend(early, place, start, q_got, kv)


def solution(mesh):
    return jax.shard_map(
        per_device,
        mesh=mesh,
        in_specs=(P(("dp", "ctx"), None), P(("dp", "ctx"), None), P(("dp", "ctx")), P("dp", "ctx")),
        out_specs=P(("dp", "ctx"), None),
        check_vma=False,
    )
```
